512 devices in a mesh: land: 128 (over y, z, core), cam: 4 (over x).
Axes of the slice: x: 4, y: 8, z: 8, core: 2. Of those that a mesh axis runs over, the one named last changes fastest.
Arguments:
- jac_cam: float32 [2, 15, 4, 262144], P(None, None, None, ('land', 'cam')), may hold values from -6 to 6
- jac_land: float32 [2, 3, 4, 262144], P(None, None, None, ('land', 'cam')), may hold values from -6 to 6
- land_damp: float32 [3, 262144], P(None, ('land', 'cam')), may hold values from 0.5 to 4
- obs_slot: int32 [4, 262144], P(None, ('land', 'cam')), may hold values from 0 to 4095
- tile_count: int32 [512], P(('land', 'cam')), may hold values from 1 to 4, as said below
- send_list: int32 [512, 4096], P(('land', 'cam')), may hold values from 0 to 1023
- rhs: float32 [15, 131072], P(None, ('land', 'cam')), may hold values from -6 to 6
- precond: float32 [15, 15, 131072], P(None, None, ('land', 'cam')), as said below
- cam_damp: float32 [15, 131072], P(None, ('land', 'cam')), may hold values from 0.5 to 4
Outputs:
- camera_step: float32 [15, 131072], P(None, ('land', 'cam'))
- residual: float32 [15, 131072], P(None, ('land', 'cam'))
The draws below stay inside these ranges and needn't reach their ends.
Inputs may be any that keep to these rules, and one draw needn't show every extreme that they name: obs_slot[k, l] // 32 is the owner group of the observed camera and obs_slot[k, l] mod 32 its entry in that group's list for the observing device. `send_list`: entry i * 32 + e, with e < 32, of a device's row is a position among its land index's 1024 cameras, ordered by index on cam; the same camera may appear more than once. `tile_count`: some device holds 4 live tiles in every draw. `precond`: each camera's block is symmetric positive definite.
All inputs are finite; a program needn't handle non-finite values.
Results may differ from the reference program's by a relative error of at most 0.00055.
Values sent between devices are 32-bit elements; how exact they have to be, the bound alone decides.
A program may use at most 64 MiB of HBM per device.

```python
import math
import jax
import jax.numpy as jnp

PARAMS = 15
TRACK = 4
TILE = 128
TILES_DEV = 4
CAM_DEV = 256
SEND = 32
ITERS = 2
SHARDS = 512
GROUP = 1024
LANDMARKS = 262144
CAMERAS = 131072
SLOTS = 4096
N_CAM = 4


def draw_tile_count(key, part):
    key = jax.random.fold_in(key, 11)
    count_key, full_key = jax.random.split(key)
    counts = jax.random.randint(count_key, (SHARDS,), 1, TILES_DEV + 1)
    fullest = jax.random.randint(full_key, (), 0, SHARDS)
    return jnp.where(jnp.arange(SHARDS) == fullest, TILES_DEV, counts).astype(jnp.int32)


def draw_precond(key, part):
    key = jax.random.fold_in(key, 23)
    side_key, diag_key = jax.random.split(key)
    spread = jax.random.uniform(side_key, (PARAMS, PARAMS, CAMERAS), jnp.float32, -0.04, 0.04)
    spread = 0.5 * (spread + jnp.transpose(spread, (1, 0, 2)))
    diagonal = jnp.exp(jax.random.uniform(diag_key, (PARAMS, CAMERAS), jnp.float32, math.log(0.6), math.log(3.0)))
    identity = (jnp.arange(PARAMS)[:, None] == jnp.arange(PARAMS)[None, :]).astype(jnp.float32)
    return spread * (1.0 - identity)[:, :, None] + identity[:, :, None] * diagonal[None, :, :]


def set_ends(array, stream_key, low, high):
    longest = array.shape.index(max(array.shape))
    spots = []
    for shift in (0, 1):
        where = [jax.random.randint(jax.random.fold_in(stream_key, axis), (), 0, length) for axis, length in enumerate(array.shape)]
        where[longest] = (where[longest] + shift) % array.shape[longest]
        spots.append(tuple(where))
    return array.at[spots[0]].set(low).at[spots[1]].set(high)


def block_levels(rng, extent, cuts, low, top_value):
    loudness = 1.0
    for dim, blocks in cuts:
        steps = jax.random.uniform(jax.random.fold_in(jax.random.fold_in(rng, 6), dim), (blocks,), jnp.float32, low / len(cuts), top_value / len(cuts))
        loudness = loudness * jnp.repeat(jnp.exp(steps), extent[dim] // blocks).reshape((-1,) + (1,) * (len(extent) - 1 - dim))
    return loudness


def scatter_about(rng, shape, scale, bound, cuts=(), held_as=jnp.bfloat16):
    result = jax.random.normal(rng, shape, jnp.float32) * scale
    if len(cuts) > 0:
        result = block_levels(rng, shape, cuts, -0.22, 0.18) * result
    return jnp.clip(result, min=-bound, max=bound).astype(held_as)


def setup_inputs(seed: int = 0) -> dict:
    streams_of = jax.random.split(jax.random.key(seed), 10)
    jac_cam = scatter_about(streams_of[0], (2, PARAMS, TRACK, LANDMARKS), 1.0, 6.0, ((3, 512),), jnp.float32)
    jac_land = scatter_about(streams_of[1], (2, 3, TRACK, LANDMARKS), 1.0, 6.0, ((3, 512),), jnp.float32)
    land_damp = jnp.clip(jnp.exp(math.log(4.0) - 2.0794415 * jax.random.uniform(streams_of[2], (3, LANDMARKS), jnp.float32) ** block_levels(streams_of[2], (3, LANDMARKS), ((1, 512),), -0.2, 0.2)), 0.5, 4.0)
    obs_slot = set_ends(jax.random.randint(streams_of[3], (TRACK, LANDMARKS), 0, SLOTS), jax.random.fold_in(streams_of[3], 1), 0, SLOTS - 1).astype(jnp.int32)
    tile_count = draw_tile_count(jax.random.fold_in(streams_of[9], 71), 0)
    send_list = set_ends(jax.random.randint(streams_of[5], (SHARDS, SLOTS), 0, GROUP), jax.random.fold_in(streams_of[5], 1), 0, GROUP - 1).astype(jnp.int32)
    rhs = scatter_about(streams_of[6], (PARAMS, CAMERAS), 1.0, 6.0, ((1, 512),), jnp.float32)
    precond = draw_precond(jax.random.fold_in(streams_of[9], 71), 0)
    cam_damp = jnp.clip(jnp.exp(math.log(4.0) - 2.0794415 * jax.random.uniform(streams_of[8], (PARAMS, CAMERAS), jnp.float32) ** block_levels(streams_of[8], (PARAMS, CAMERAS), ((1, 512),), -0.2, 0.2)), 0.5, 4.0)
    return {"jac_cam": jac_cam, "jac_land": jac_land, "land_damp": land_damp, "obs_slot": obs_slot, "tile_count": tile_count, "send_list": send_list, "rhs": rhs, "precond": precond, "cam_damp": cam_damp}


def invert_three(matrix):
    adjugate = [[None, None, None], [None, None, None], [None, None, None]]
    for row_ix in range(3):
        for col_ix in range(3):
            next_row = (col_ix + 1) % 3
            last_row = (col_ix + 2) % 3
            next_col = (row_ix + 1) % 3
            last_col = (row_ix + 2) % 3
            adjugate[row_ix][col_ix] = (matrix[next_row][next_col] * matrix[last_row][last_col]
                                        - matrix[next_row][last_col] * matrix[last_row][next_col])
    determinant = matrix[0][0] * adjugate[0][0] + matrix[0][1] * adjugate[1][0] + matrix[0][2] * adjugate[2][0]
    return [[adjugate[row_ix][col_ix] / determinant for col_ix in range(3)] for row_ix in range(3)]


def landmark_blocks(land_jacobian, land_damp):
    matrix = []
    for row_ix in range(3):
        entries = []
        for col_ix in range(3):
            entry = jnp.sum(land_jacobian[:, row_ix] * land_jacobian[:, col_ix], axis=(0, 1))
            if row_ix == col_ix:
                entry = entry + land_damp[row_ix]
            entries.append(entry)
        matrix.append(entries)
    return matrix


def apply_inverse(inverse, vector):
    return jnp.stack([inverse[row_ix][0] * vector[0] + inverse[row_ix][1] * vector[1] + inverse[row_ix][2] * vector[2]
                      for row_ix in range(3)])


def precondition(blocks, vector):
    return jnp.sum(blocks * vector[None], axis=1)


def reference(jac_cam, jac_land, land_damp, obs_slot, tile_count, send_list, rhs, precond, cam_damp):
    lm_dev = TILES_DEV * TILE
    position = jnp.arange(LANDMARKS, dtype=jnp.int32)
    owner = position // lm_dev
    live = ((position % lm_dev) // TILE < tile_count[owner]).astype(jnp.float32)
    cam_jacobian = jac_cam * live
    land_jacobian = jac_land * live
    land_row = owner // N_CAM
    cam_col = owner % N_CAM
    source = obs_slot // SEND
    sender = source * N_CAM + cam_col[None, :]
    column = land_row[None, :] * SEND + obs_slot % SEND
    camera_id = source * (CAM_DEV * N_CAM) + send_list[sender, column]
    flat_ids = camera_id.reshape(-1)
    inverse = invert_three(landmark_blocks(land_jacobian, land_damp))

    def operate(direction):
        gathered = direction[:, camera_id]
        predicted = jnp.sum(cam_jacobian * gathered[None], axis=1)
        land_rhs = jnp.sum(land_jacobian * predicted[:, None], axis=(0, 2))
        land_step = apply_inverse(inverse, land_rhs)
        misfit = predicted - jnp.sum(land_jacobian * land_step[None, :, None], axis=1)
        cam_terms = jnp.sum(cam_jacobian * misfit[:, None], axis=0)
        totals = jnp.zeros((PARAMS, CAMERAS), jnp.float32).at[:, flat_ids].add(cam_terms.reshape(PARAMS, -1))
        return totals + cam_damp * direction

    camera_step = jnp.zeros((PARAMS, CAMERAS), jnp.float32)
    residual = rhs
    smoothed = precondition(precond, residual)
    direction = smoothed
    energy = jnp.sum(residual * smoothed)
    for iteration in range(ITERS):
        product = operate(direction)
        stride = energy / jnp.sum(direction * product)
        camera_step = camera_step + stride * direction
        residual = residual - stride * product
        smoothed = precondition(precond, residual)
        energy_new = jnp.sum(residual * smoothed)
        direction = smoothed + (energy_new / energy) * direction
        energy = energy_new
    return camera_step, residual
```

```python
import jax
import jax.numpy as jnp
from jax import lax
from jax.experimental import pallas as pl
from jax.experimental.pallas import tpu as pltpu
from jax.sharding import PartitionSpec as P

MESH = pl.DeviceIdType.MESH
F32 = jnp.float32
BF16 = jnp.bfloat16
PARAMS = 15
N_LAND = 128
N_CAM = 4
NT = (((1,), (1,)), ((), ()))


def split(value):
    head = value.astype(BF16)
    return head, (value - head.astype(F32)).astype(BF16)


def total(value):
    return jnp.sum(jnp.sum(value, axis=1, keepdims=True), axis=0, keepdims=True)


def pick(row, lane):
    lanes = lax.broadcasted_iota(jnp.int32, row.shape, 1)
    return jnp.sum(jnp.where(lanes == lane, row, 0.0), axis=1, keepdims=True)


def scalar_row(scalars, width):
    lanes = lax.broadcasted_iota(jnp.int32, (1, width), 1)
    row = jnp.zeros((1, width), F32)
    for lane, value in enumerate(scalars):
        row = jnp.where(lanes == lane, value, row)
    return row


def put_scalars(chunk, scalars):
    rows = lax.broadcasted_iota(jnp.int32, chunk.shape, 0)
    for m, value in enumerate(scalars):
        chunk = jnp.where(rows == 16 * m + 15, value, chunk)
    return chunk


def take_scalars(chunk, count):
    return [jnp.sum(chunk[16 * m + 15 : 16 * m + 16, :], axis=1, keepdims=True) for m in range(count)]


def place(k):
    return 4 + (1 - 2 * lax.rem(k, 2)) * lax.div(k + 1, 2)


def kernel(
    tiles, jac_cam, jac_land, land_damp, obs_slot, send_list, rhs, precond, cam_damp,
    step_out, residual_out,
    hot_cam, hot_slot, owner_of, listed, entry_of, jac, land, inverse, seen, spread, owned,
    ag, gs, rr, xs, xr,
    land_send, land_recv, cam_send, cam_recv,
):
    me = lax.axis_index("land")
    cam = lax.axis_index("cam")
    me_y, me_z, me_c = lax.div(me, 16), lax.rem(lax.div(me, 2), 8), lax.rem(me, 2)

    def mixed(index):
        return lax.rem(index, 4) * 32 + lax.div(index, 4)

    def each_land_peer(action):
        for total_steps in range(14):
            first = max(0, total_steps - 7)

            def body(ky, carry, total_steps=total_steps):
                y = lax.rem(me_y + place(ky), 8)
                z = lax.rem(me_z + place(total_steps - ky), 8)
                base = y * 16 + z * 2
                action(base + me_c)
                action(base + 1 - me_c)
                return carry

            lax.fori_loop(first, min(7, total_steps) + 1, body, 0)
        action(me + 1 - 2 * me_c)

    def cam_peers():
        return [lax.rem(cam + hop, N_CAM) for hop in (2, 1, 3)]

    barrier = pltpu.get_barrier_semaphore()
    for peer in cam_peers():
        pl.semaphore_signal(barrier, inc=1, device_id={"cam": peer}, device_id_type=MESH)
    each_land_peer(
        lambda peer: pl.semaphore_signal(barrier, inc=1, device_id={"land": peer}, device_id_type=MESH)
    )

    def land_start(n, forward):
        if forward:
            source, target = mixed, me
            own = mixed(me)
        else:
            source, target = (lambda index: index), mixed(me)
            own = me
        xr[n, target] = xs[n, own]

        def send(peer):
            pltpu.make_async_remote_copy(
                src_ref=xs.at[n, source(peer)],
                dst_ref=xr.at[n, target],
                send_sem=land_send.at[n],
                recv_sem=land_recv.at[n],
                device_id={"land": peer},
                device_id_type=MESH,
            ).start()

        each_land_peer(send)

    def land_wait(n, sem):
        rows = pl.ds(0, N_LAND - 1)
        pltpu.make_async_copy(xs.at[n, rows], xr.at[n, rows], sem.at[n]).wait()

    def cam_start(n, source, target):
        for peer in cam_peers():
            pltpu.make_async_remote_copy(
                src_ref=source(peer),
                dst_ref=target,
                send_sem=cam_send.at[n],
                recv_sem=cam_recv.at[n],
                device_id={"cam": peer},
                device_id_type=MESH,
            ).start()

    def cam_wait(n, sem):
        rows = pl.ds(0, N_CAM - 1)
        pltpu.make_async_copy(gs.at[0, rows], rr.at[0, rows], sem.at[n]).wait()

    def precondition(vector):
        result = precond[0] * vector[0:1]
        for b in range(1, PARAMS):
            result = result + precond[b] * vector[b : b + 1]
        return result

    def gather_start(it, direction, scalars):
        ag[it, cam] = jnp.concatenate([direction, scalar_row(scalars, 256)], axis=0)
        return lambda: cam_start(2 * it, lambda peer: ag.at[it, cam], ag.at[it, cam])

    def make_hot_cam():
        listing = jnp.concatenate([send_list[...], jnp.zeros((96, 128), jnp.int32)], axis=0)
        turned = jnp.transpose(listing)
        entries = turned[0:32]
        for i in range(1, 4):
            entries = entries + pltpu.roll(turned[32 * i : 32 * i + 32], 32 * i, 1)
        owner_of[...] = lax.shift_right_logical(entries, 8)
        listed[...] = lax.bitwise_and(entries, 255)
        rows = lax.broadcasted_iota(jnp.int32, (256, 128), 0)
        for e in range(32):
            hot_cam[:, e * 128 : e * 128 + 128] = jnp.where(rows == listed[e : e + 1, :], 1.0, 0.0).astype(BF16)

    def make_hot_slot():
        slots = obs_slot[...]
        group, entry = lax.shift_right_logical(slots, 5), lax.bitwise_and(slots, 31)
        place_of = lax.shift_right_logical(entry, 4) * 128 + group
        entry_of[...] = lax.bitwise_and(entry, 15)
        rows = lax.broadcasted_iota(jnp.int32, (256, 512), 0)
        for k in range(4):
            hot_slot[:, k * 512 : k * 512 + 512] = jnp.where(rows == place_of[k : k + 1, :], 1.0, 0.0).astype(BF16)

    def live_lanes():
        lanes = lax.broadcasted_iota(jnp.int32, (1, 512), 1)
        return jnp.where(lax.shift_right_logical(lanes, 7) < tiles[0], 1.0, 0.0)

    def make_jac():
        live = live_lanes()
        for r in range(2):
            for k in range(4):
                block = jac_cam[r, :, k, :] * live
                jac[r, :, k * 512 : k * 512 + 512] = jnp.concatenate([block, jnp.zeros((1, 512), F32)], axis=0)

    def make_land():
        live = live_lanes()
        for b in range(3):
            land[b] = jnp.concatenate([jac_land[0, b], jac_land[1, b]], axis=0) * live
        blocks = [[None] * 3 for _ in range(3)]
        for b in range(3):
            for d in range(b, 3):
                entry = jnp.sum(land[b] * land[d], axis=0, keepdims=True)
                if b == d:
                    entry = entry + land_damp[b : b + 1, :]
                blocks[b][d] = blocks[d][b] = entry
        adjugate = [[None] * 3 for _ in range(3)]
        for b in range(3):
            for d in range(3):
                b1, b2, d1, d2 = (d + 1) % 3, (d + 2) % 3, (b + 1) % 3, (b + 2) % 3
                adjugate[b][d] = blocks[b1][d1] * blocks[b2][d2] - blocks[b1][d2] * blocks[b2][d1]
        determinant = sum(blocks[0][d] * adjugate[d][0] for d in range(3))
        for b in range(3):
            for d in range(3):
                inverse[3 * b + d : 3 * b + d + 1, :] = adjugate[b][d] / determinant

    def send_listed(n, it, scalars):
        head, tail = split(ag[it].reshape(64, 256))
        both = jnp.concatenate([head, tail], axis=0)
        columns = []
        for pair in range(16):
            product = jnp.dot(both, hot_cam[:, pair * 256 : pair * 256 + 256], preferred_element_type=F32)
            product = product[0:64] + product[64:128]
            for half in range(2):
                e = 2 * pair + half
                owner = owner_of[e : e + 1, :]
                part = product[:, half * 128 : half * 128 + 128]
                chosen = part[0:16]
                for j in range(1, 4):
                    chosen = jnp.where(owner == j, part[16 * j : 16 * j + 16], chosen)
                columns.append(chosen)
        for quarter in range(4):
            chunk = jnp.concatenate(columns[8 * quarter : 8 * quarter + 8], axis=0)
            if quarter == 0:
                chunk = put_scalars(chunk, scalars)
            xs[n, :, quarter, :] = jnp.transpose(chunk)
        land_start(n, True)

    def observed(n, count):
        turned = [jnp.transpose(xr[n, :, quarter, :]) for quarter in range(4)]
        scalars = take_scalars(turned[0], count)
        slots = jnp.concatenate(
            [jnp.concatenate([turned[0], turned[2]], axis=1), jnp.concatenate([turned[1], turned[3]], axis=1)], axis=0
        )
        head, tail = split(slots)
        both = jnp.concatenate([head, tail], axis=0)
        columns = []
        for pair in range(8):
            product = jnp.dot(both, hot_slot[:, pair * 256 : pair * 256 + 256], preferred_element_type=F32)
            product = product[0:256] + product[256:512]
            for half in range(2):
                k, lane = divmod((2 * pair + half) * 128, 512)
                entry = entry_of[k : k + 1, lane : lane + 128]
                part = product[:, half * 128 : half * 128 + 128]
                chosen = part[0:16]
                for e in range(1, 16):
                    chosen = jnp.where(entry == e, part[16 * e : 16 * e + 16], chosen)
                columns.append(chosen)
        return jnp.concatenate(columns, axis=1), scalars

    def eliminate(gathered):
        rows = []
        for r in range(2):
            for k in range(4):
                lanes = slice(k * 512, k * 512 + 512)
                rows.append(jnp.sum(jac[r, :, lanes] * gathered[:, lanes], axis=0, keepdims=True))
        predicted = jnp.concatenate(rows, axis=0)
        land_rhs = [jnp.sum(land[b] * predicted, axis=0, keepdims=True) for b in range(3)]
        misfit = predicted
        for b in range(3):
            step = sum(inverse[3 * b + d : 3 * b + d + 1, :] * land_rhs[d] for d in range(3))
            misfit = misfit - land[b] * step
        terms = []
        for k in range(4):
            lanes = slice(k * 512, k * 512 + 512)
            terms.append(jac[0, :, lanes] * misfit[k : k + 1] + jac[1, :, lanes] * misfit[4 + k : 5 + k])
        return jnp.concatenate(terms, axis=1), total(predicted * misfit)

    def send_terms(n, terms, scalars):
        head = terms.astype(BF16).astype(F32)
        tail = terms - head
        for k in range(4):
            lanes = slice(k * 512, k * 512 + 512)
            entry = entry_of[k : k + 1, :]
            for e in range(16):
                mask = entry == e
                spread[16 * e : 16 * e + 16, lanes] = jnp.where(mask, head[:, lanes], 0.0).astype(BF16)
                spread[256 + 16 * e : 272 + 16 * e, lanes] = jnp.where(mask, tail[:, lanes], 0.0).astype(BF16)
        sums = lax.dot_general(spread[...], hot_slot[...], NT, preferred_element_type=F32)
        sums = sums[0:256] + sums[256:512]
        for quarter in range(4):
            row, lane = 128 * (quarter % 2), 128 * (quarter // 2)
            chunk = sums[row : row + 128, lane : lane + 128]
            if quarter == 0:
                chunk = put_scalars(chunk, scalars)
            xs[n, :, quarter, :] = jnp.transpose(chunk)
        land_start(n, False)

    def group_sums(n, it, count):
        scalars = []
        for quarter in range(4):
            turned = jnp.transpose(xr[n, :, quarter, :])
            if quarter == 0:
                scalars = take_scalars(turned, count)
            head = turned.astype(BF16).astype(F32)
            tail = turned - head
            for e8 in range(8):
                e = 8 * quarter + e8
                lanes = slice(e * 128, e * 128 + 128)
                owner = owner_of[e : e + 1, :]
                for j in range(4):
                    mask = owner == j
                    rows = slice(16 * e8, 16 * e8 + 16)
                    owned[16 * j : 16 * j + 16, lanes] = jnp.where(mask, head[rows], 0.0).astype(BF16)
                    owned[64 + 16 * j : 80 + 16 * j, lanes] = jnp.where(mask, tail[rows], 0.0).astype(BF16)
        sums = lax.dot_general(owned[...], hot_cam[...], NT, preferred_element_type=F32)
        sums = sums[0:64] + sums[64:128]
        if count:
            rows = lax.broadcasted_iota(jnp.int32, sums.shape, 0)
            sums = jnp.where(lax.bitwise_and(rows, 15) == 15, scalar_row(scalars, 256), sums)
        gs[it] = sums.reshape(4, 16, 256)
        rr[it, cam] = gs[it, cam]
        cam_start(2 * it + 1, lambda peer: gs.at[it, peer], rr.at[it, cam])

    def own_sums(it):
        return rr[it, 0] + rr[it, 1] + rr[it, 2] + rr[it, 3]

    start = rhs[...]
    smoothed = precondition(start)
    send = gather_start(0, smoothed, [])
    make_hot_cam()
    pl.semaphore_wait(barrier, N_LAND - 1 + N_CAM - 1)
    send()
    make_hot_slot()
    make_jac()
    cam_wait(0, cam_recv)
    send_listed(0, 0, [])
    make_land()
    energy = total(start * smoothed)
    land_wait(0, land_recv)
    gathered, _ = observed(0, 0)
    seen[...] = gathered
    terms, _ = eliminate(gathered)
    send_terms(1, terms, [])
    land_wait(1, land_recv)
    group_sums(1, 0, 0)
    cam_wait(1, cam_recv)
    product = own_sums(0)[0:PARAMS] + cam_damp[...] * smoothed

    turned = precondition(product)
    scalars = [energy, total(smoothed * product), total(start * turned), total(product * turned)]
    gather_start(1, turned, scalars)()
    cam_wait(2, cam_recv)
    row = ag[1, 0, 15:16] + ag[1, 1, 15:16] + ag[1, 2, 15:16] + ag[1, 3, 15:16]
    send_listed(2, 1, [pick(row, lane) for lane in range(4)])
    land_wait(2, land_recv)
    gathered, (energy, curve, cross, square) = observed(2, 4)
    stride = energy / curve
    energy_new = energy - stride * (cross + curve) + stride * stride * square
    beta = energy_new / energy
    terms, curve = eliminate((1.0 + beta) * seen[...] - stride * gathered)
    residual = start - stride * product
    smoothed_new = smoothed - stride * turned
    direction = smoothed_new + beta * smoothed
    damped = cam_damp[...] * direction
    send_terms(3, terms, [total(residual * smoothed_new), curve + total(damped * direction)])
    land_wait(3, land_recv)
    group_sums(3, 1, 2)
    cam_wait(3, cam_recv)
    sums = own_sums(1)
    energy, curve = pick(sums[15:16], 0), pick(sums[15:16], 1)
    stride_new = energy / curve
    step_out[...] = stride * smoothed + stride_new * direction
    residual_out[...] = residual - stride_new * (sums[0:PARAMS] + damped)
    for n in range(4):
        land_wait(n, land_send)
        cam_wait(n, cam_send)


def local(jac_cam, jac_land, land_damp, obs_slot, tile_count, send_list, rhs, precond, cam_damp):
    vmem = pl.BlockSpec(memory_space=pltpu.VMEM)
    out = jax.ShapeDtypeStruct((PARAMS, 256), F32)
    return pl.pallas_call(
        kernel,
        out_shape=(out, out),
        in_specs=[pl.BlockSpec(memory_space=pltpu.SMEM)] + [vmem] * 8,
        out_specs=(vmem, vmem),
        scratch_shapes=[
            pltpu.VMEM((256, 4096), BF16),
            pltpu.VMEM((256, 2048), BF16),
            pltpu.VMEM((32, 128), jnp.int32),
            pltpu.VMEM((32, 128), jnp.int32),
            pltpu.VMEM((4, 512), jnp.int32),
            pltpu.VMEM((2, 16, 2048), F32),
            pltpu.VMEM((3, 8, 512), F32),
            pltpu.VMEM((9, 512), F32),
            pltpu.VMEM((16, 2048), F32),
            pltpu.VMEM((512, 2048), BF16),
            pltpu.VMEM((128, 4096), BF16),
            pltpu.VMEM((2, 4, 16, 256), F32),
            pltpu.VMEM((2, 4, 16, 256), F32),
            pltpu.VMEM((2, 4, 16, 256), F32),
            pltpu.VMEM((4, N_LAND, 4, 128), F32),
            pltpu.VMEM((4, N_LAND, 4, 128), F32),
            pltpu.SemaphoreType.DMA((4,)),
            pltpu.SemaphoreType.DMA((4,)),
            pltpu.SemaphoreType.DMA((4,)),
            pltpu.SemaphoreType.DMA((4,)),
        ],
        compiler_params=pltpu.CompilerParams(
            collective_id=0, has_side_effects=True, vmem_limit_bytes=48 * 1024 * 1024
        ),
    )(tile_count, jac_cam, jac_land, land_damp, obs_slot, send_list.reshape(32, 128), rhs, precond, cam_damp)


def solution(mesh):
    whole = ("land", "cam")
    return jax.shard_map(
        local,
        mesh=mesh,
        in_specs=(
            P(None, None, None, whole),
            P(None, None, None, whole),
            P(None, whole),
            P(None, whole),
            P(whole),
            P(whole, None),
            P(None, whole),
            P(None, None, whole),
            P(None, whole),
        ),
        out_specs=(P(None, whole), P(None, whole)),
        check_vma=False,
    )
```

```python
import jax
import jax.numpy as jnp
from jax import lax
from jax.experimental import pallas as pl
from jax.experimental.pallas import tpu as pltpu
from jax.sharding import PartitionSpec as P

MESH = pl.DeviceIdType.MESH
F32 = jnp.float32
BF16 = jnp.bfloat16
PARAMS = 15
N_LAND = 128
N_CAM = 4


def split(value):
    head = value.astype(BF16)
    return head, (value - head.astype(F32)).astype(BF16)


def total(value):
    return jnp.sum(jnp.sum(value, axis=1, keepdims=True), axis=0, keepdims=True)


def pick(row, lane):
    lanes = lax.broadcasted_iota(jnp.int32, row.shape, 1)
    return jnp.sum(jnp.where(lanes == lane, row, 0.0), axis=1, keepdims=True)


def scalar_row(scalars, width):
    lanes = lax.broadcasted_iota(jnp.int32, (1, width), 1)
    row = jnp.zeros((1, width), F32)
    for lane, value in enumerate(scalars):
        row = jnp.where(lanes == lane, value, row)
    return row


def put_scalars(chunk, scalars):
    rows = lax.broadcasted_iota(jnp.int32, chunk.shape, 0)
    for m, value in enumerate(scalars):
        chunk = jnp.where(rows == 16 * m + 15, value, chunk)
    return chunk


def take_scalars(chunk, count):
    return [jnp.sum(chunk[16 * m + 15 : 16 * m + 16, :], axis=1, keepdims=True) for m in range(count)]


def kernel(
    tiles_in, jac_cam_in, jac_land_in, land_damp_in, obs_slot_in, send_list_in, rhs_in, precond_in, cam_damp_in,
    both_out,
    tiles, jac_cam, jac_land, land_damp, obs_slot, send_list, group_rhs, group_precond, group_damp,
    hot_cam, hot_slot, hot_cam_t, hot_slot_t, in_owner, in_entry, owner_of, listed, entry_of, slot_place, jac, land, inverse,
    seen, spread, owned,
    ag, parts, products, gs, rr, xs, xr,
    land_send, land_recv, cam_send, cam_recv, fetch_sem,
):
    me = lax.axis_index("land")
    cam = lax.axis_index("cam")
    me_y, me_z, me_c = lax.div(me, 16), lax.rem(lax.div(me, 2), 8), lax.rem(me, 2)

    def mixed(index):
        return lax.rem(index, 4) * 32 + lax.div(index, 4)

    ring = (4, 3, 5, 2, 6, 1, 7, 0)
    at_y = [lax.rem(me_y + step, 8) * 16 + me_c for step in range(8)]
    at_z = [lax.rem(me_z + step, 8) * 2 for step in range(8)]
    other = 1 - 2 * me_c

    def each_land_peer(action):
        for far in range(14):
            for k in range(max(0, far - 7), min(7, far) + 1):
                peer = at_y[ring[k]] + at_z[ring[far - k]]
                action(peer)
                action(peer + other)
        action(me + other)

    def cam_peers():
        return [lax.rem(cam + hop, N_CAM) for hop in (2, 1, 3)]

    pairs = (
        (rhs_in, group_rhs.at[cam]),
        (precond_in, group_precond.at[cam]),
        (send_list_in, send_list),
        (obs_slot_in, obs_slot),
        (tiles_in, tiles),
        (jac_cam_in, jac_cam),
        (jac_land_in, jac_land),
        (land_damp_in, land_damp),
        (cam_damp_in, group_damp.at[cam]),
    )
    fetches = [pltpu.make_async_copy(source, target, fetch_sem.at[n]) for n, (source, target) in enumerate(pairs)]
    for fetch in fetches:
        fetch.start()

    barrier = pltpu.get_barrier_semaphore()
    for peer in cam_peers():
        pl.semaphore_signal(barrier, inc=1, device_id={"cam": peer}, device_id_type=MESH)
    each_land_peer(
        lambda peer: pl.semaphore_signal(barrier, inc=1, device_id={"land": peer}, device_id_type=MESH)
    )

    def land_start(n, forward):
        if forward:
            source, target = mixed, me
            own = mixed(me)
        else:
            source, target = (lambda index: index), mixed(me)
            own = me
        xr[n, target] = xs[n, own]

        def send(peer):
            pltpu.make_async_remote_copy(
                src_ref=xs.at[n, source(peer)],
                dst_ref=xr.at[n, target],
                send_sem=land_send.at[n],
                recv_sem=land_recv.at[n],
                device_id={"land": peer},
                device_id_type=MESH,
            ).start()

        each_land_peer(send)

    def land_wait(n, sem):
        rows = pl.ds(0, N_LAND - 1)
        pltpu.make_async_copy(xs.at[n, rows], xr.at[n, rows], sem.at[n]).wait()

    def cam_start(n, source, target):
        for peer in cam_peers():
            pltpu.make_async_remote_copy(
                src_ref=source(peer),
                dst_ref=target,
                send_sem=cam_send.at[n],
                recv_sem=cam_recv.at[n],
                device_id={"cam": peer},
                device_id_type=MESH,
            ).start()

    cam_buffers = (ag.at[0], parts, rr, group_precond, group_damp, group_rhs)

    def cam_share(n):
        row = cam_buffers[n].at[cam]
        cam_start(n, lambda peer: row, row)

    def cam_wait(n, sem):
        rows = cam_buffers[n].at[pl.ds(0, N_CAM - 1)]
        pltpu.make_async_copy(rows, rows, sem.at[n]).wait()

    def precondition(owner, vector):
        result = group_precond[owner, 0] * vector[0:1]
        for b in range(1, PARAMS):
            result = result + group_precond[owner, b] * vector[b : b + 1]
        return result

    def padded(vector):
        return jnp.concatenate([vector, jnp.zeros((1, 256), F32)], axis=0)

    def make_hot_cam():
        listing = jnp.concatenate([send_list[...], jnp.zeros((96, 128), jnp.int32)], axis=0)
        turned = jnp.transpose(listing)
        entries = turned[0:32]
        for i in range(1, 4):
            entries = entries + pltpu.roll(turned[32 * i : 32 * i + 32], 32 * i, 1)
        owner_of[...] = lax.shift_right_logical(entries, 8)
        listed[...] = lax.bitwise_and(entries, 255)
        rows = lax.broadcasted_iota(jnp.int32, (256, 128), 0)
        for e in range(32):
            hot_cam[:, e * 128 : e * 128 + 128] = jnp.where(rows == listed[e : e + 1, :], 1.0, 0.0).astype(BF16)

    def hot_columns(row):
        column = jnp.transpose(jnp.broadcast_to(row, (128, 128)))
        lanes = lax.broadcasted_iota(jnp.int32, (128, 128), 1)
        halves = [jnp.where(lanes + shift == column, 1.0, 0.0) for shift in (0, 128)]
        return jnp.concatenate(halves, axis=1).astype(BF16)

    def make_cam_masks():
        for e in range(32):
            lanes = slice(e * 128, e * 128 + 128)
            hot_cam_t[lanes, :] = hot_columns(listed[e : e + 1, :])
            owner = jnp.broadcast_to(owner_of[e : e + 1, :], (16, 128))
            for j in range(4):
                in_owner[16 * j : 16 * j + 16, lanes] = jnp.where(owner == j, 1.0, 0.0).astype(BF16)

    def make_hot_slot():
        slots = obs_slot[...]
        group, entry = lax.shift_right_logical(slots, 5), lax.bitwise_and(slots, 31)
        place_of = lax.shift_right_logical(entry, 4) * 128 + group
        entry_of[...] = lax.bitwise_and(entry, 15)
        rows = lax.broadcasted_iota(jnp.int32, (256, 512), 0)
        for k in range(4):
            hot_slot[:, k * 512 : k * 512 + 512] = jnp.where(rows == place_of[k : k + 1, :], 1.0, 0.0).astype(BF16)
            slot_place[k : k + 1, :] = place_of[k : k + 1, :]

    def make_slot_masks():
        for k in range(4):
            for part in range(4):
                lanes = slice(part * 128, part * 128 + 128)
                both = slice(k * 512 + part * 128, k * 512 + part * 128 + 128)
                hot_slot_t[both, :] = hot_columns(slot_place[k : k + 1, lanes])
                entry = jnp.broadcast_to(entry_of[k : k + 1, lanes], (16, 128))
                for e in range(16):
                    in_entry[16 * e : 16 * e + 16, both] = jnp.where(entry == e, 1.0, 0.0).astype(BF16)

    def live_lanes():
        lanes = lax.broadcasted_iota(jnp.int32, (1, 512), 1)
        return jnp.where(lax.shift_right_logical(lanes, 7) < tiles[...], 1.0, 0.0)

    def make_jac():
        live = live_lanes()
        for r in range(2):
            for k in range(4):
                block = jac_cam[r, :, k, :] * live
                jac[r, :, k * 512 : k * 512 + 512] = jnp.concatenate([block, jnp.zeros((1, 512), F32)], axis=0)

    def make_land():
        live = live_lanes()
        for b in range(3):
            land[b] = jnp.concatenate([jac_land[0, b], jac_land[1, b]], axis=0) * live
        blocks = [[None] * 3 for _ in range(3)]
        for b in range(3):
            for d in range(b, 3):
                entry = jnp.sum(land[b] * land[d], axis=0, keepdims=True)
                if b == d:
                    entry = entry + land_damp[b : b + 1, :]
                blocks[b][d] = blocks[d][b] = entry
        adjugate = [[None] * 3 for _ in range(3)]
        for b in range(3):
            for d in range(3):
                b1, b2, d1, d2 = (d + 1) % 3, (d + 2) % 3, (b + 1) % 3, (b + 2) % 3
                adjugate[b][d] = blocks[b1][d1] * blocks[b2][d2] - blocks[b1][d2] * blocks[b2][d1]
        determinant = sum(blocks[0][d] * adjugate[d][0] for d in range(3))
        for b in range(3):
            for d in range(3):
                inverse[3 * b + d : 3 * b + d + 1, :] = adjugate[b][d] / determinant

    def send_listed(n, it, scalars):
        head, tail = split(ag[it].reshape(64, 256))
        both = jnp.concatenate([head, tail], axis=0)
        columns = []
        for pair in range(16):
            product = jnp.dot(both, hot_cam[:, pair * 256 : pair * 256 + 256], preferred_element_type=F32)
            product = product[0:64] + product[64:128]
            for half in range(2):
                e = 2 * pair + half
                owner = owner_of[e : e + 1, :]
                part = product[:, half * 128 : half * 128 + 128]
                chosen = part[0:16]
                for j in range(1, 4):
                    chosen = jnp.where(owner == j, part[16 * j : 16 * j + 16], chosen)
                columns.append(chosen)
        for quarter in range(4):
            chunk = jnp.concatenate(columns[8 * quarter : 8 * quarter + 8], axis=0)
            if quarter == 0:
                chunk = put_scalars(chunk, scalars)
            xs[n, :, quarter, :] = jnp.transpose(chunk)
        land_start(n, True)

    def observed(n, count):
        turned = [jnp.transpose(xr[n, :, quarter, :]) for quarter in range(4)]
        scalars = take_scalars(turned[0], count)
        slots = jnp.concatenate(
            [jnp.concatenate([turned[0], turned[2]], axis=1), jnp.concatenate([turned[1], turned[3]], axis=1)], axis=0
        )
        head, tail = split(slots)
        both = jnp.concatenate([head, tail], axis=0)
        columns = []
        for pair in range(8):
            product = jnp.dot(both, hot_slot[:, pair * 256 : pair * 256 + 256], preferred_element_type=F32)
            product = product[0:256] + product[256:512]
            for half in range(2):
                k, lane = divmod((2 * pair + half) * 128, 512)
                entry = entry_of[k : k + 1, lane : lane + 128]
                part = product[:, half * 128 : half * 128 + 128]
                chosen = part[0:16]
                for e in range(1, 16):
                    chosen = jnp.where(entry == e, part[16 * e : 16 * e + 16], chosen)
                columns.append(chosen)
        return jnp.concatenate(columns, axis=1), scalars

    def eliminate(gathered):
        rows = []
        for r in range(2):
            for k in range(4):
                lanes = slice(k * 512, k * 512 + 512)
                rows.append(jnp.sum(jac[r, :, lanes] * gathered[:, lanes], axis=0, keepdims=True))
        predicted = jnp.concatenate(rows, axis=0)
        land_rhs = [jnp.sum(land[b] * predicted, axis=0, keepdims=True) for b in range(3)]
        misfit = predicted
        for b in range(3):
            step = sum(inverse[3 * b + d : 3 * b + d + 1, :] * land_rhs[d] for d in range(3))
            misfit = misfit - land[b] * step
        terms = []
        for k in range(4):
            lanes = slice(k * 512, k * 512 + 512)
            terms.append(jac[0, :, lanes] * misfit[k : k + 1] + jac[1, :, lanes] * misfit[4 + k : 5 + k])
        return jnp.concatenate(terms, axis=1), total(predicted * misfit)

    def send_terms(n, terms, scalars):
        head, tail = split(terms)
        for e in range(16):
            mask = in_entry[16 * e : 16 * e + 16, :]
            spread[16 * e : 16 * e + 16, :] = head * mask
            spread[256 + 16 * e : 272 + 16 * e, :] = tail * mask
        sums = jnp.dot(spread[...], hot_slot_t[...], preferred_element_type=F32)
        sums = sums[0:256] + sums[256:512]
        for quarter in range(4):
            row, lane = 128 * (quarter % 2), 128 * (quarter // 2)
            chunk = sums[row : row + 128, lane : lane + 128]
            if quarter == 0:
                chunk = put_scalars(chunk, scalars)
            xs[n, :, quarter, :] = jnp.transpose(chunk)
        land_start(n, False)

    def group_sums(n, count):
        scalars = []
        for quarter in range(4):
            turned = jnp.transpose(xr[n, :, quarter, :])
            if quarter == 0:
                scalars = take_scalars(turned, count)
            head, tail = split(turned)
            for e8 in range(8):
                lanes = slice(1024 * quarter + e8 * 128, 1024 * quarter + e8 * 128 + 128)
                rows = slice(16 * e8, 16 * e8 + 16)
                for j in range(4):
                    mask = in_owner[16 * j : 16 * j + 16, lanes]
                    owned[16 * j : 16 * j + 16, lanes] = head[rows] * mask
                    owned[64 + 16 * j : 80 + 16 * j, lanes] = tail[rows] * mask
        sums = jnp.dot(owned[...], hot_cam_t[...], preferred_element_type=F32)
        sums = sums[0:64] + sums[64:128]
        if count:
            rows = lax.broadcasted_iota(jnp.int32, sums.shape, 0)
            sums = jnp.where(lax.bitwise_and(rows, 15) == 15, scalar_row(scalars, 256), sums)
        return sums.reshape(4, 16, 256)

    fetches[0].wait()
    fetches[1].wait()
    ag[0, cam] = padded(precondition(cam, group_rhs[cam]))
    pl.semaphore_wait(barrier, N_LAND - 1 + N_CAM - 1)
    cam_share(0)
    fetches[2].wait()
    make_hot_cam()
    for fetch in fetches[3:]:
        fetch.wait()
    make_hot_slot()
    make_jac()
    cam_wait(0, cam_recv)
    send_listed(0, 0, [])
    for n in (3, 4, 5):
        cam_share(n)
    make_land()
    make_slot_masks()
    make_cam_masks()
    land_wait(0, land_recv)
    gathered, _ = observed(0, 0)
    seen[...] = gathered
    terms, _ = eliminate(gathered)
    send_terms(1, terms, [])
    land_wait(1, land_recv)
    parts[cam] = group_sums(1, 0)
    cam_share(1)
    for n in (3, 4, 5):
        cam_wait(n, cam_recv)
    cam_wait(1, cam_recv)

    sums = [jnp.zeros((PARAMS, 256), F32)] * 4
    for j in range(N_CAM):
        start, smoothed = group_rhs[j], ag[0, j, 0:PARAMS]
        product = parts[0, j, 0:PARAMS] + parts[1, j, 0:PARAMS] + parts[2, j, 0:PARAMS] + parts[3, j, 0:PARAMS]
        product = product + group_damp[j] * smoothed
        turned = precondition(j, product)
        products[j] = product
        ag[1, j] = padded(turned)
        pairs = ((start, smoothed), (smoothed, product), (start, turned), (product, turned))
        sums = [value + left * right for value, (left, right) in zip(sums, pairs)]
    send_listed(2, 1, [total(value) for value in sums])
    land_wait(2, land_recv)
    gathered, (energy, curve, cross, square) = observed(2, 4)
    stride = energy / curve
    energy_new = energy - stride * (cross + curve) + stride * stride * square
    beta = energy_new / energy
    terms, curve = eliminate((1.0 + beta) * seen[...] - stride * gathered)
    smoothed = ag[0, cam, 0:PARAMS]
    residual = group_rhs[cam] - stride * products[cam]
    smoothed_new = smoothed - stride * ag[1, cam, 0:PARAMS]
    direction = smoothed_new + beta * smoothed
    damped = group_damp[cam] * direction
    send_terms(3, terms, [total(residual * smoothed_new), curve + total(damped * direction)])
    land_wait(3, land_recv)
    gs[...] = group_sums(3, 2)
    rr[cam] = gs[cam]
    cam_start(2, lambda peer: gs.at[peer], rr.at[cam])
    cam_wait(2, cam_recv)
    sums = rr[0] + rr[1] + rr[2] + rr[3]
    energy, curve = pick(sums[15:16], 0), pick(sums[15:16], 1)
    stride_new = energy / curve
    both_out[0] = stride * smoothed + stride_new * direction
    both_out[1] = residual - stride_new * (sums[0:PARAMS] + damped)
    for n in range(4):
        land_wait(n, land_send)
    for n in range(6):
        cam_wait(n, cam_send)


def local(jac_cam, jac_land, land_damp, obs_slot, tile_count, send_list, rhs, precond, cam_damp):
    vmem = pl.BlockSpec(memory_space=pltpu.VMEM)
    both = pl.pallas_call(
        kernel,
        out_shape=jax.ShapeDtypeStruct((2, PARAMS, 256), F32),
        in_specs=[pl.BlockSpec(memory_space=pl.ANY)] * 9,
        out_specs=vmem,
        scratch_shapes=[
            pltpu.VMEM((1, 1), jnp.int32),
            pltpu.VMEM((2, PARAMS, 4, 512), F32),
            pltpu.VMEM((2, 3, 4, 512), F32),
            pltpu.VMEM((3, 512), F32),
            pltpu.VMEM((4, 512), jnp.int32),
            pltpu.VMEM((32, 128), jnp.int32),
            pltpu.VMEM((N_CAM, PARAMS, 256), F32),
            pltpu.VMEM((N_CAM, PARAMS, PARAMS, 256), F32),
            pltpu.VMEM((N_CAM, PARAMS, 256), F32),
            pltpu.VMEM((256, 4096), BF16),
            pltpu.VMEM((256, 2048), BF16),
            pltpu.VMEM((4096, 256), BF16),
            pltpu.VMEM((2048, 256), BF16),
            pltpu.VMEM((64, 4096), BF16),
            pltpu.VMEM((256, 2048), BF16),
            pltpu.VMEM((32, 128), jnp.int32),
            pltpu.VMEM((32, 128), jnp.int32),
            pltpu.VMEM((4, 512), jnp.int32),
            pltpu.VMEM((4, 512), jnp.int32),
            pltpu.VMEM((2, 16, 2048), F32),
            pltpu.VMEM((3, 8, 512), F32),
            pltpu.VMEM((9, 512), F32),
            pltpu.VMEM((16, 2048), F32),
            pltpu.VMEM((512, 2048), BF16),
            pltpu.VMEM((128, 4096), BF16),
            pltpu.VMEM((2, 4, 16, 256), F32),
            pltpu.VMEM((N_CAM, N_CAM, 16, 256), F32),
            pltpu.VMEM((N_CAM, PARAMS, 256), F32),
            pltpu.VMEM((N_CAM, 16, 256), F32),
            pltpu.VMEM((N_CAM, 16, 256), F32),
            pltpu.VMEM((4, N_LAND, 4, 128), F32),
            pltpu.VMEM((4, N_LAND, 4, 128), F32),
            pltpu.SemaphoreType.DMA((4,)),
            pltpu.SemaphoreType.DMA((4,)),
            pltpu.SemaphoreType.DMA((6,)),
            pltpu.SemaphoreType.DMA((6,)),
            pltpu.SemaphoreType.DMA((9,)),
        ],
        compiler_params=pltpu.CompilerParams(
            collective_id=0, has_side_effects=True, vmem_limit_bytes=60 * 1024 * 1024
        ),
    )(tile_count.reshape(1, 1), jac_cam, jac_land, land_damp, obs_slot, send_list.reshape(32, 128), rhs, precond, cam_damp)
    return both[0], both[1]


def solution(mesh):
    whole = ("land", "cam")
    return jax.shard_map(
        local,
        mesh=mesh,
        in_specs=(
            P(None, None, None, whole),
            P(None, None, None, whole),
            P(None, whole),
            P(None, whole),
            P(whole),
            P(whole, None),
            P(None, whole),
            P(None, None, whole),
            P(None, whole),
        ),
        out_specs=(P(None, whole), P(None, whole)),
        check_vma=False,
    )
```

```python
import jax
import jax.numpy as jnp
from jax import lax
from jax.experimental import pallas as pl
from jax.experimental.pallas import tpu as pltpu
from jax.sharding import PartitionSpec as P

MESH = pl.DeviceIdType.MESH
F32 = jnp.float32
BF16 = jnp.bfloat16
PARAMS = 15
N_LAND = 128
N_CAM = 4


def split(value):
    head = value.astype(BF16)
    return head, (value - head.astype(F32)).astype(BF16)


def total(value):
    return jnp.sum(jnp.sum(value, axis=1, keepdims=True), axis=0, keepdims=True)


def pick(row, lane):
    lanes = lax.broadcasted_iota(jnp.int32, row.shape, 1)
    return jnp.sum(jnp.where(lanes == lane, row, 0.0), axis=1, keepdims=True)


def scalar_row(scalars, width):
    lanes = lax.broadcasted_iota(jnp.int32, (1, width), 1)
    row = jnp.zeros((1, width), F32)
    for lane, value in enumerate(scalars):
        row = jnp.where(lanes == lane, value, row)
    return row


def put_scalars(chunk, scalars):
    rows = lax.broadcasted_iota(jnp.int32, chunk.shape, 0)
    for m, value in enumerate(scalars):
        chunk = jnp.where(rows == 16 * m + 15, value, chunk)
    return chunk


def take_scalars(chunk, count):
    return [jnp.sum(chunk[16 * m + 15 : 16 * m + 16, :], axis=1, keepdims=True) for m in range(count)]


def kernel(
    tiles_in, jac_cam_in, jac_land_in, land_damp_in, obs_slot_in, send_list_in, rhs_in, precond_in, cam_damp_in,
    both_out,
    tiles, jac_cam, jac_land, land_damp, obs_slot, send_list, group_rhs, group_precond, group_damp,
    hot_cam, hot_slot, hot_cam_t, hot_slot_t, in_owner, in_entry, owner_of, listed, entry_of, slot_place, jac, land, inverse,
    seen, owned,
    ag, parts, products, gs, rr, xs, xr,
    land_send, land_recv, cam_send, cam_recv, fetch_sem,
):
    me = lax.axis_index("land")
    cam = lax.axis_index("cam")
    me_y, me_z, me_c = lax.div(me, 16), lax.rem(lax.div(me, 2), 8), lax.rem(me, 2)

    def mixed(index):
        return lax.rem(index, 4) * 32 + lax.div(index, 4)

    ring = (4, 3, 5, 2, 6, 1, 7, 0)
    at_y = [lax.rem(me_y + step, 8) * 16 + me_c for step in range(8)]
    at_z = [lax.rem(me_z + step, 8) * 2 for step in range(8)]
    other = 1 - 2 * me_c

    def each_land_peer(action):
        for far in range(14):
            for k in range(max(0, far - 7), min(7, far) + 1):
                peer = at_y[ring[k]] + at_z[ring[far - k]]
                action(peer)
                action(peer + other)
        action(me + other)

    def cam_peers():
        return [lax.rem(cam + hop, N_CAM) for hop in (2, 1, 3)]

    pairs = (
        (rhs_in, group_rhs.at[cam]),
        (precond_in, group_precond.at[cam]),
        (send_list_in, send_list),
        (obs_slot_in, obs_slot),
        (tiles_in, tiles),
        (jac_cam_in, jac_cam),
        (jac_land_in, jac_land),
        (land_damp_in, land_damp),
        (cam_damp_in, group_damp.at[cam]),
    )
    fetches = [pltpu.make_async_copy(source, target, fetch_sem.at[n]) for n, (source, target) in enumerate(pairs)]
    for fetch in fetches:
        fetch.start()

    barrier = pltpu.get_barrier_semaphore()
    for peer in cam_peers():
        pl.semaphore_signal(barrier, inc=1, device_id={"cam": peer}, device_id_type=MESH)
    each_land_peer(
        lambda peer: pl.semaphore_signal(barrier, inc=1, device_id={"land": peer}, device_id_type=MESH)
    )

    def land_start(n, forward):
        if forward:
            source, target = mixed, me
            own = mixed(me)
        else:
            source, target = (lambda index: index), mixed(me)
            own = me
        xr[n, target] = xs[n, own]

        def send(peer):
            pltpu.make_async_remote_copy(
                src_ref=xs.at[n, source(peer)],
                dst_ref=xr.at[n, target],
                send_sem=land_send.at[n],
                recv_sem=land_recv.at[n],
                device_id={"land": peer},
                device_id_type=MESH,
            ).start()

        each_land_peer(send)

    def land_wait(n, sem):
        rows = pl.ds(0, N_LAND - 1)
        pltpu.make_async_copy(xs.at[n, rows], xr.at[n, rows], sem.at[n]).wait()

    def cam_start(n, source, target):
        for peer in cam_peers():
            pltpu.make_async_remote_copy(
                src_ref=source(peer),
                dst_ref=target,
                send_sem=cam_send.at[n],
                recv_sem=cam_recv.at[n],
                device_id={"cam": peer},
                device_id_type=MESH,
            ).start()

    cam_buffers = (ag.at[0], parts, rr, group_precond, group_damp, group_rhs)

    def cam_share(n):
        row = cam_buffers[n].at[cam]
        cam_start(n, lambda peer: row, row)

    def cam_wait(n, sem):
        rows = cam_buffers[n].at[pl.ds(0, N_CAM - 1)]
        pltpu.make_async_copy(rows, rows, sem.at[n]).wait()

    def precondition(owner, vector):
        result = group_precond[owner, 0] * vector[0:1]
        for b in range(1, PARAMS):
            result = result + group_precond[owner, b] * vector[b : b + 1]
        return result

    def padded(vector):
        return jnp.concatenate([vector, jnp.zeros((1, 256), F32)], axis=0)

    def make_hot_cam():
        listing = jnp.concatenate([send_list[...], jnp.zeros((96, 128), jnp.int32)], axis=0)
        turned = jnp.transpose(listing)
        entries = turned[0:32]
        for i in range(1, 4):
            entries = entries + pltpu.roll(turned[32 * i : 32 * i + 32], 32 * i, 1)
        owner_of[...] = lax.shift_right_logical(entries, 8)
        listed[...] = lax.bitwise_and(entries, 255)
        rows = lax.broadcasted_iota(jnp.int32, (256, 128), 0)
        for e in range(32):
            hot_cam[:, e * 128 : e * 128 + 128] = jnp.where(rows == listed[e : e + 1, :], 1.0, 0.0).astype(BF16)

    def hot_columns(row):
        column = jnp.transpose(jnp.broadcast_to(row, (128, 128)))
        lanes = lax.broadcasted_iota(jnp.int32, (128, 128), 1)
        halves = [jnp.where(lanes + shift == column, 1.0, 0.0) for shift in (0, 128)]
        return jnp.concatenate(halves, axis=1).astype(BF16)

    def make_cam_masks():
        for e in range(32):
            lanes = slice(e * 128, e * 128 + 128)
            hot_cam_t[lanes, :] = hot_columns(listed[e : e + 1, :])
            owner = jnp.broadcast_to(owner_of[e : e + 1, :], (16, 128))
            for j in range(4):
                in_owner[16 * j : 16 * j + 16, lanes] = jnp.where(owner == j, 1.0, 0.0).astype(BF16)

    def make_hot_slot():
        slots = obs_slot[...]
        group, entry = lax.shift_right_logical(slots, 5), lax.bitwise_and(slots, 31)
        place_of = lax.shift_right_logical(entry, 4) * 128 + group
        entry_of[...] = lax.bitwise_and(entry, 15)
        rows = lax.broadcasted_iota(jnp.int32, (256, 512), 0)
        for k in range(4):
            hot_slot[:, k * 512 : k * 512 + 512] = jnp.where(rows == place_of[k : k + 1, :], 1.0, 0.0).astype(BF16)
            slot_place[k : k + 1, :] = place_of[k : k + 1, :]

    def make_slot_masks():
        for k in range(4):
            for part in range(4):
                lanes = slice(part * 128, part * 128 + 128)
                both = slice(k * 512 + part * 128, k * 512 + part * 128 + 128)
                hot_slot_t[both, :] = hot_columns(slot_place[k : k + 1, lanes])
                entry = jnp.broadcast_to(entry_of[k : k + 1, lanes], (16, 128))
                for e in range(16):
                    in_entry[16 * e : 16 * e + 16, both] = jnp.where(entry == e, 1.0, 0.0).astype(BF16)

    def live_lanes():
        lanes = lax.broadcasted_iota(jnp.int32, (1, 512), 1)
        return jnp.where(lax.shift_right_logical(lanes, 7) < tiles[...], 1.0, 0.0)

    def make_jac():
        live = live_lanes()
        for r in range(2):
            for k in range(4):
                block = jac_cam[r, :, k, :] * live
                jac[r, :, k * 512 : k * 512 + 512] = jnp.concatenate([block, jnp.zeros((1, 512), F32)], axis=0)

    def make_land():
        live = live_lanes()
        for b in range(3):
            land[b] = jnp.concatenate([jac_land[0, b], jac_land[1, b]], axis=0) * live
        blocks = [[None] * 3 for _ in range(3)]
        for b in range(3):
            for d in range(b, 3):
                entry = jnp.sum(land[b] * land[d], axis=0, keepdims=True)
                if b == d:
                    entry = entry + land_damp[b : b + 1, :]
                blocks[b][d] = blocks[d][b] = entry
        adjugate = [[None] * 3 for _ in range(3)]
        for b in range(3):
            for d in range(3):
                b1, b2, d1, d2 = (d + 1) % 3, (d + 2) % 3, (b + 1) % 3, (b + 2) % 3
                adjugate[b][d] = blocks[b1][d1] * blocks[b2][d2] - blocks[b1][d2] * blocks[b2][d1]
        determinant = sum(blocks[0][d] * adjugate[d][0] for d in range(3))
        for b in range(3):
            for d in range(3):
                inverse[3 * b + d : 3 * b + d + 1, :] = adjugate[b][d] / determinant

    def send_listed(n, it, scalars):
        head, tail = split(ag[it].reshape(64, 256))
        both = jnp.concatenate([head, tail], axis=0)
        columns = []
        for pair in range(16):
            product = jnp.dot(both, hot_cam[:, pair * 256 : pair * 256 + 256], preferred_element_type=F32)
            product = product[0:64] + product[64:128]
            for half in range(2):
                e = 2 * pair + half
                owner = owner_of[e : e + 1, :]
                part = product[:, half * 128 : half * 128 + 128]
                chosen = part[0:16]
                for j in range(1, 4):
                    chosen = jnp.where(owner == j, part[16 * j : 16 * j + 16], chosen)
                columns.append(chosen)
        for quarter in range(4):
            chunk = jnp.concatenate(columns[8 * quarter : 8 * quarter + 8], axis=0)
            if quarter == 0:
                chunk = put_scalars(chunk, scalars)
            xs[n, :, quarter, :] = jnp.transpose(chunk)
        land_start(n, True)

    def observed(n, count):
        turned = [jnp.transpose(xr[n, :, quarter, :]) for quarter in range(4)]
        scalars = take_scalars(turned[0], count)
        slots = jnp.concatenate(
            [jnp.concatenate([turned[0], turned[2]], axis=1), jnp.concatenate([turned[1], turned[3]], axis=1)], axis=0
        )
        head, tail = split(slots)
        columns = []
        for pair in range(8):
            hot = hot_slot[:, pair * 256 : pair * 256 + 256]
            product = jnp.dot(head, hot, preferred_element_type=F32) + jnp.dot(tail, hot, preferred_element_type=F32)
            for half in range(2):
                k, lane = divmod((2 * pair + half) * 128, 512)
                entry = entry_of[k : k + 1, lane : lane + 128]
                part = product[:, half * 128 : half * 128 + 128]
                chosen = part[0:16]
                for e in range(1, 16):
                    chosen = jnp.where(entry == e, part[16 * e : 16 * e + 16], chosen)
                columns.append(chosen)
        return jnp.concatenate(columns, axis=1), scalars

    def eliminate(gathered):
        rows = []
        for r in range(2):
            for k in range(4):
                lanes = slice(k * 512, k * 512 + 512)
                rows.append(jnp.sum(jac[r, :, lanes] * gathered[:, lanes], axis=0, keepdims=True))
        predicted = jnp.concatenate(rows, axis=0)
        land_rhs = [jnp.sum(land[b] * predicted, axis=0, keepdims=True) for b in range(3)]
        misfit = predicted
        for b in range(3):
            step = sum(inverse[3 * b + d : 3 * b + d + 1, :] * land_rhs[d] for d in range(3))
            misfit = misfit - land[b] * step
        terms = []
        for k in range(4):
            lanes = slice(k * 512, k * 512 + 512)
            terms.append(jac[0, :, lanes] * misfit[k : k + 1] + jac[1, :, lanes] * misfit[4 + k : 5 + k])
        return jnp.concatenate(terms, axis=1), total(predicted * misfit)

    def send_terms(n, terms, scalars):
        head, tail = split(terms)
        for half in range(2):
            sums = jnp.zeros((256, 256), F32)
            for k in range(4):
                lanes = slice(k * 512, k * 512 + 512)
                block = []
                for part in (head, tail):
                    for e in range(8 * half, 8 * half + 8):
                        block.append(part[:, lanes] * in_entry[16 * e : 16 * e + 16, lanes])
                block = jnp.concatenate(block, axis=0)
                sums = sums + jnp.dot(block, hot_slot_t[lanes, :], preferred_element_type=F32)
            sums = sums[0:128] + sums[128:256]
            for eb in range(2):
                chunk = sums[:, 128 * eb : 128 * eb + 128]
                if eb + half == 0:
                    chunk = put_scalars(chunk, scalars)
                xs[n, :, half + 2 * eb, :] = jnp.transpose(chunk)
        land_start(n, False)

    def group_sums(n, count):
        scalars = []
        for quarter in range(4):
            turned = jnp.transpose(xr[n, :, quarter, :])
            if quarter == 0:
                scalars = take_scalars(turned, count)
            head, tail = split(turned)
            for e8 in range(8):
                lanes = slice(1024 * quarter + e8 * 128, 1024 * quarter + e8 * 128 + 128)
                rows = slice(16 * e8, 16 * e8 + 16)
                for j in range(4):
                    mask = in_owner[16 * j : 16 * j + 16, lanes]
                    owned[16 * j : 16 * j + 16, lanes] = head[rows] * mask
                    owned[64 + 16 * j : 80 + 16 * j, lanes] = tail[rows] * mask
        sums = jnp.dot(owned[...], hot_cam_t[...], preferred_element_type=F32)
        sums = sums[0:64] + sums[64:128]
        if count:
            rows = lax.broadcasted_iota(jnp.int32, sums.shape, 0)
            sums = jnp.where(lax.bitwise_and(rows, 15) == 15, scalar_row(scalars, 256), sums)
        return sums.reshape(4, 16, 256)

    fetches[0].wait()
    fetches[1].wait()
    ag[0, cam] = padded(precondition(cam, group_rhs[cam]))
    pl.semaphore_wait(barrier, N_LAND - 1 + N_CAM - 1)
    cam_share(0)
    fetches[2].wait()
    make_hot_cam()
    for fetch in fetches[3:]:
        fetch.wait()
    make_hot_slot()
    make_jac()
    cam_wait(0, cam_recv)
    send_listed(0, 0, [])
    for n in (3, 4, 5):
        cam_share(n)
    make_land()
    make_slot_masks()
    make_cam_masks()
    land_wait(0, land_recv)
    gathered, _ = observed(0, 0)
    seen[...] = gathered
    terms, _ = eliminate(gathered)
    send_terms(1, terms, [])
    land_wait(1, land_recv)
    parts[cam] = group_sums(1, 0)
    cam_share(1)
    for n in (3, 4, 5):
        cam_wait(n, cam_recv)
    cam_wait(1, cam_recv)

    sums = [jnp.zeros((PARAMS, 256), F32)] * 4
    for j in range(N_CAM):
        start, smoothed = group_rhs[j], ag[0, j, 0:PARAMS]
        product = parts[0, j, 0:PARAMS] + parts[1, j, 0:PARAMS] + parts[2, j, 0:PARAMS] + parts[3, j, 0:PARAMS]
        product = product + group_damp[j] * smoothed
        turned = precondition(j, product)
        products[j] = product
        ag[1, j] = padded(turned)
        pairs = ((start, smoothed), (smoothed, product), (start, turned), (product, turned))
        sums = [value + left * right for value, (left, right) in zip(sums, pairs)]
    send_listed(2, 1, [total(value) for value in sums])
    land_wait(2, land_recv)
    gathered, (energy, curve, cross, square) = observed(2, 4)
    stride = energy / curve
    energy_new = energy - stride * (cross + curve) + stride * stride * square
    beta = energy_new / energy
    terms, curve = eliminate((1.0 + beta) * seen[...] - stride * gathered)
    smoothed = ag[0, cam, 0:PARAMS]
    residual = group_rhs[cam] - stride * products[cam]
    smoothed_new = smoothed - stride * ag[1, cam, 0:PARAMS]
    direction = smoothed_new + beta * smoothed
    damped = group_damp[cam] * direction
    send_terms(3, terms, [total(residual * smoothed_new), curve + total(damped * direction)])
    land_wait(3, land_recv)
    gs[...] = group_sums(3, 2)
    rr[cam] = gs[cam]
    cam_start(2, lambda peer: gs.at[peer], rr.at[cam])
    cam_wait(2, cam_recv)
    sums = rr[0] + rr[1] + rr[2] + rr[3]
    energy, curve = pick(sums[15:16], 0), pick(sums[15:16], 1)
    stride_new = energy / curve
    both_out[0] = stride * smoothed + stride_new * direction
    both_out[1] = residual - stride_new * (sums[0:PARAMS] + damped)
    for n in range(4):
        land_wait(n, land_send)
    for n in range(6):
        cam_wait(n, cam_send)


def local(jac_cam, jac_land, land_damp, obs_slot, tile_count, send_list, rhs, precond, cam_damp):
    vmem = pl.BlockSpec(memory_space=pltpu.VMEM)
    both = pl.pallas_call(
        kernel,
        out_shape=jax.ShapeDtypeStruct((2, PARAMS, 256), F32),
        in_specs=[pl.BlockSpec(memory_space=pl.ANY)] * 9,
        out_specs=vmem,
        scratch_shapes=[
            pltpu.VMEM((1, 1), jnp.int32),
            pltpu.VMEM((2, PARAMS, 4, 512), F32),
            pltpu.VMEM((2, 3, 4, 512), F32),
            pltpu.VMEM((3, 512), F32),
            pltpu.VMEM((4, 512), jnp.int32),
            pltpu.VMEM((32, 128), jnp.int32),
            pltpu.VMEM((N_CAM, PARAMS, 256), F32),
            pltpu.VMEM((N_CAM, PARAMS, PARAMS, 256), F32),
            pltpu.VMEM((N_CAM, PARAMS, 256), F32),
            pltpu.VMEM((256, 4096), BF16),
            pltpu.VMEM((256, 2048), BF16),
            pltpu.VMEM((4096, 256), BF16),
            pltpu.VMEM((2048, 256), BF16),
            pltpu.VMEM((64, 4096), BF16),
            pltpu.VMEM((256, 2048), BF16),
            pltpu.VMEM((32, 128), jnp.int32),
            pltpu.VMEM((32, 128), jnp.int32),
            pltpu.VMEM((4, 512), jnp.int32),
            pltpu.VMEM((4, 512), jnp.int32),
            pltpu.VMEM((2, 16, 2048), F32),
            pltpu.VMEM((3, 8, 512), F32),
            pltpu.VMEM((9, 512), F32),
            pltpu.VMEM((16, 2048), F32),
            pltpu.VMEM((128, 4096), BF16),
            pltpu.VMEM((2, 4, 16, 256), F32),
            pltpu.VMEM((N_CAM, N_CAM, 16, 256), F32),
            pltpu.VMEM((N_CAM, PARAMS, 256), F32),
            pltpu.VMEM((N_CAM, 16, 256), F32),
            pltpu.VMEM((N_CAM, 16, 256), F32),
            pltpu.VMEM((4, N_LAND, 4, 128), F32),
            pltpu.VMEM((4, N_LAND, 4, 128), F32),
            pltpu.SemaphoreType.DMA((4,)),
            pltpu.SemaphoreType.DMA((4,)),
            pltpu.SemaphoreType.DMA((6,)),
            pltpu.SemaphoreType.DMA((6,)),
            pltpu.SemaphoreType.DMA((9,)),
        ],
        compiler_params=pltpu.CompilerParams(
            collective_id=0, has_side_effects=True, vmem_limit_bytes=60 * 1024 * 1024
        ),
    )(tile_count.reshape(1, 1), jac_cam, jac_land, land_damp, obs_slot, send_list.reshape(32, 128), rhs, precond, cam_damp)
    return both[0], both[1]


def solution(mesh):
    whole = ("land", "cam")
    return jax.shard_map(
        local,
        mesh=mesh,
        in_specs=(
            P(None, None, None, whole),
            P(None, None, None, whole),
            P(None, whole),
            P(None, whole),
            P(whole),
            P(whole, None),
            P(None, whole),
            P(None, None, whole),
            P(None, whole),
        ),
        out_specs=(P(None, whole), P(None, whole)),
        check_vma=False,
    )
```

```python
import jax
import jax.numpy as jnp
from jax import lax
from jax.experimental import pallas as pl
from jax.experimental.pallas import tpu as pltpu
from jax.sharding import PartitionSpec as P

MESH = pl.DeviceIdType.MESH
F32 = jnp.float32
BF16 = jnp.bfloat16
PARAMS = 15
N_LAND = 128
N_CAM = 4


def split(value):
    head = value.astype(BF16)
    return head, (value - head.astype(F32)).astype(BF16)


def total(value):
    return jnp.sum(jnp.sum(value, axis=1, keepdims=True), axis=0, keepdims=True)


def pick(row, lane):
    lanes = lax.broadcasted_iota(jnp.int32, row.shape, 1)
    return jnp.sum(jnp.where(lanes == lane, row, 0.0), axis=1, keepdims=True)


def scalar_row(scalars, width):
    lanes = lax.broadcasted_iota(jnp.int32, (1, width), 1)
    row = jnp.zeros((1, width), F32)
    for lane, value in enumerate(scalars):
        row = jnp.where(lanes == lane, value, row)
    return row


def put_scalars(chunk, scalars):
    rows = lax.broadcasted_iota(jnp.int32, chunk.shape, 0)
    for m, value in enumerate(scalars):
        chunk = jnp.where(rows == 16 * m + 15, value, chunk)
    return chunk


def take_scalars(chunk, count):
    return [jnp.sum(chunk[16 * m + 15 : 16 * m + 16, :], axis=1, keepdims=True) for m in range(count)]


def kernel(
    tiles_in, jac_cam_in, jac_land_in, land_damp_in, obs_slot_in, send_list_in, rhs_in, precond_in, cam_damp_in,
    both_out,
    tiles, jac_cam, jac_land, land_damp, obs_slot, send_list, group_rhs, group_precond, group_damp,
    hot_cam, hot_slot, hot_cam_t, hot_slot_t, in_owner, in_entry, owner_of, listed, entry_of, slot_place, jac, land, inverse,
    seen,
    ag, parts, products, gs, rr, xs, xr,
    land_send, land_recv, cam_send, cam_recv, fetch_sem,
):
    me = lax.axis_index("land")
    cam = lax.axis_index("cam")
    me_y, me_z, me_c = lax.div(me, 16), lax.rem(lax.div(me, 2), 8), lax.rem(me, 2)

    def mixed(index):
        return lax.rem(index, 4) * 32 + lax.div(index, 4)

    ring = (4, 3, 5, 2, 6, 1, 7, 0)
    at_y = [lax.rem(me_y + step, 8) * 16 + me_c for step in range(8)]
    at_z = [lax.rem(me_z + step, 8) * 2 for step in range(8)]
    other = 1 - 2 * me_c

    def each_land_peer(action):
        for far in range(14):
            for k in range(max(0, far - 7), min(7, far) + 1):
                peer = at_y[ring[k]] + at_z[ring[far - k]]
                action(peer)
                action(peer + other)
        action(me + other)

    def cam_peers():
        return [lax.rem(cam + hop, N_CAM) for hop in (2, 1, 3)]

    pairs = (
        (rhs_in, group_rhs.at[cam]),
        (precond_in, group_precond.at[cam]),
        (send_list_in, send_list),
        (obs_slot_in, obs_slot),
        (tiles_in, tiles),
        (jac_cam_in, jac_cam),
        (jac_land_in, jac_land),
        (land_damp_in, land_damp),
        (cam_damp_in, group_damp.at[cam]),
    )
    fetches = [pltpu.make_async_copy(source, target, fetch_sem.at[n]) for n, (source, target) in enumerate(pairs)]
    for fetch in fetches:
        fetch.start()

    barrier = pltpu.get_barrier_semaphore()
    for peer in cam_peers():
        pl.semaphore_signal(barrier, inc=1, device_id={"cam": peer}, device_id_type=MESH)
    each_land_peer(
        lambda peer: pl.semaphore_signal(barrier, inc=1, device_id={"land": peer}, device_id_type=MESH)
    )

    def land_start(n, forward):
        if forward:
            source, target = mixed, me
            own = mixed(me)
        else:
            source, target = (lambda index: index), mixed(me)
            own = me
        xr[n, target] = xs[n, own]

        def send(peer):
            pltpu.make_async_remote_copy(
                src_ref=xs.at[n, source(peer)],
                dst_ref=xr.at[n, target],
                send_sem=land_send.at[n],
                recv_sem=land_recv.at[n],
                device_id={"land": peer},
                device_id_type=MESH,
            ).start()

        each_land_peer(send)

    def land_wait(n, sem):
        rows = pl.ds(0, N_LAND - 1)
        pltpu.make_async_copy(xs.at[n, rows], xr.at[n, rows], sem.at[n]).wait()

    def cam_start(n, source, target):
        for peer in cam_peers():
            pltpu.make_async_remote_copy(
                src_ref=source(peer),
                dst_ref=target,
                send_sem=cam_send.at[n],
                recv_sem=cam_recv.at[n],
                device_id={"cam": peer},
                device_id_type=MESH,
            ).start()

    cam_buffers = (ag.at[0], parts, rr, group_precond, group_damp, group_rhs)

    def cam_share(n):
        row = cam_buffers[n].at[cam]
        cam_start(n, lambda peer: row, row)

    def cam_wait(n, sem):
        rows = cam_buffers[n].at[pl.ds(0, N_CAM - 1)]
        pltpu.make_async_copy(rows, rows, sem.at[n]).wait()

    def precondition(owner, vector):
        result = group_precond[owner, 0] * vector[0:1]
        for b in range(1, PARAMS):
            result = result + group_precond[owner, b] * vector[b : b + 1]
        return result

    def padded(vector):
        return jnp.concatenate([vector, jnp.zeros((1, 256), F32)], axis=0)

    def make_hot_cam():
        listing = jnp.concatenate([send_list[...], jnp.zeros((96, 128), jnp.int32)], axis=0)
        turned = jnp.transpose(listing)
        entries = turned[0:32]
        for i in range(1, 4):
            entries = entries + pltpu.roll(turned[32 * i : 32 * i + 32], 32 * i, 1)
        owner_of[...] = lax.shift_right_logical(entries, 8)
        listed[...] = lax.bitwise_and(entries, 255)
        rows = lax.broadcasted_iota(jnp.int32, (256, 128), 0)
        for e in range(32):
            hot_cam[:, e * 128 : e * 128 + 128] = jnp.where(rows == listed[e : e + 1, :], 1.0, 0.0).astype(BF16)

    def hot_columns(row):
        column = jnp.transpose(jnp.broadcast_to(row, (128, 128)))
        lanes = lax.broadcasted_iota(jnp.int32, (128, 128), 1)
        halves = [jnp.where(lanes + shift == column, 1.0, 0.0) for shift in (0, 128)]
        return jnp.concatenate(halves, axis=1).astype(BF16)

    def make_cam_masks():
        for e in range(32):
            lanes = slice(e * 128, e * 128 + 128)
            hot_cam_t[lanes, :] = hot_columns(listed[e : e + 1, :])
            owner = jnp.broadcast_to(owner_of[e : e + 1, :], (16, 128))
            for j in range(4):
                in_owner[16 * j : 16 * j + 16, lanes] = jnp.where(owner == j, 1.0, 0.0).astype(BF16)

    def make_hot_slot():
        slots = obs_slot[...]
        group, entry = lax.shift_right_logical(slots, 5), lax.bitwise_and(slots, 31)
        place_of = lax.shift_right_logical(entry, 4) * 128 + group
        entry_of[...] = lax.bitwise_and(entry, 15)
        rows = lax.broadcasted_iota(jnp.int32, (256, 512), 0)
        for k in range(4):
            hot_slot[:, k * 512 : k * 512 + 512] = jnp.where(rows == place_of[k : k + 1, :], 1.0, 0.0).astype(BF16)
            slot_place[k : k + 1, :] = place_of[k : k + 1, :]

    def make_slot_masks():
        for k in range(4):
            for part in range(4):
                lanes = slice(part * 128, part * 128 + 128)
                both = slice(k * 512 + part * 128, k * 512 + part * 128 + 128)
                hot_slot_t[both, :] = hot_columns(slot_place[k : k + 1, lanes])
                entry = jnp.broadcast_to(entry_of[k : k + 1, lanes], (16, 128))
                for e in range(16):
                    in_entry[16 * e : 16 * e + 16, both] = jnp.where(entry == e, 1.0, 0.0).astype(BF16)

    def live_lanes():
        lanes = lax.broadcasted_iota(jnp.int32, (1, 512), 1)
        return jnp.where(lax.shift_right_logical(lanes, 7) < tiles[...], 1.0, 0.0)

    def make_jac():
        live = live_lanes()
        for r in range(2):
            for k in range(4):
                block = jac_cam[r, :, k, :] * live
                jac[r, :, k * 512 : k * 512 + 512] = jnp.concatenate([block, jnp.zeros((1, 512), F32)], axis=0)

    def make_land():
        live = live_lanes()
        for b in range(3):
            land[b] = jnp.concatenate([jac_land[0, b], jac_land[1, b]], axis=0) * live
        blocks = [[None] * 3 for _ in range(3)]
        for b in range(3):
            for d in range(b, 3):
                entry = jnp.sum(land[b] * land[d], axis=0, keepdims=True)
                if b == d:
                    entry = entry + land_damp[b : b + 1, :]
                blocks[b][d] = blocks[d][b] = entry
        adjugate = [[None] * 3 for _ in range(3)]
        for b in range(3):
            for d in range(3):
                b1, b2, d1, d2 = (d + 1) % 3, (d + 2) % 3, (b + 1) % 3, (b + 2) % 3
                adjugate[b][d] = blocks[b1][d1] * blocks[b2][d2] - blocks[b1][d2] * blocks[b2][d1]
        determinant = sum(blocks[0][d] * adjugate[d][0] for d in range(3))
        for b in range(3):
            for d in range(3):
                inverse[3 * b + d : 3 * b + d + 1, :] = adjugate[b][d] / determinant

    def send_listed(n, it, scalars):
        head, tail = split(ag[it].reshape(64, 256))
        both = jnp.concatenate([head, tail], axis=0)
        columns = []
        for pair in range(16):
            product = jnp.dot(both, hot_cam[:, pair * 256 : pair * 256 + 256], preferred_element_type=F32)
            product = product[0:64] + product[64:128]
            for half in range(2):
                e = 2 * pair + half
                owner = owner_of[e : e + 1, :]
                part = product[:, half * 128 : half * 128 + 128]
                chosen = part[0:16]
                for j in range(1, 4):
                    chosen = jnp.where(owner == j, part[16 * j : 16 * j + 16], chosen)
                columns.append(chosen)
        for quarter in range(4):
            chunk = jnp.concatenate(columns[8 * quarter : 8 * quarter + 8], axis=0)
            if quarter == 0:
                chunk = put_scalars(chunk, scalars)
            xs[n, :, quarter, :] = jnp.transpose(chunk)
        land_start(n, True)

    def observed(n, count):
        turned = [jnp.transpose(xr[n, :, quarter, :]) for quarter in range(4)]
        scalars = take_scalars(turned[0], count)
        slots = jnp.concatenate(
            [jnp.concatenate([turned[0], turned[2]], axis=1), jnp.concatenate([turned[1], turned[3]], axis=1)], axis=0
        )
        head, tail = split(slots)
        columns = []
        for pair in range(8):
            hot = hot_slot[:, pair * 256 : pair * 256 + 256]
            product = jnp.dot(head, hot, preferred_element_type=F32) + jnp.dot(tail, hot, preferred_element_type=F32)
            for half in range(2):
                k, lane = divmod((2 * pair + half) * 128, 512)
                entry = entry_of[k : k + 1, lane : lane + 128]
                part = product[:, half * 128 : half * 128 + 128]
                chosen = part[0:16]
                for e in range(1, 16):
                    chosen = jnp.where(entry == e, part[16 * e : 16 * e + 16], chosen)
                columns.append(chosen)
        return jnp.concatenate(columns, axis=1), scalars

    def eliminate(gathered):
        rows = []
        for r in range(2):
            for k in range(4):
                lanes = slice(k * 512, k * 512 + 512)
                rows.append(jnp.sum(jac[r, :, lanes] * gathered[:, lanes], axis=0, keepdims=True))
        predicted = jnp.concatenate(rows, axis=0)
        land_rhs = [jnp.sum(land[b] * predicted, axis=0, keepdims=True) for b in range(3)]
        misfit = predicted
        for b in range(3):
            step = sum(inverse[3 * b + d : 3 * b + d + 1, :] * land_rhs[d] for d in range(3))
            misfit = misfit - land[b] * step
        terms = []
        for k in range(4):
            lanes = slice(k * 512, k * 512 + 512)
            terms.append(jac[0, :, lanes] * misfit[k : k + 1] + jac[1, :, lanes] * misfit[4 + k : 5 + k])
        return jnp.concatenate(terms, axis=1), total(predicted * misfit)

    def send_terms(n, terms, scalars):
        head, tail = split(terms)
        for half in range(2):
            sums = jnp.zeros((256, 256), F32)
            for k in range(4):
                lanes = slice(k * 512, k * 512 + 512)
                block = []
                for part in (head, tail):
                    for e in range(8 * half, 8 * half + 8):
                        block.append(part[:, lanes] * in_entry[16 * e : 16 * e + 16, lanes])
                block = jnp.concatenate(block, axis=0)
                sums = sums + jnp.dot(block, hot_slot_t[lanes, :], preferred_element_type=F32)
            sums = sums[0:128] + sums[128:256]
            for eb in range(2):
                chunk = sums[:, 128 * eb : 128 * eb + 128]
                if eb + half == 0:
                    chunk = put_scalars(chunk, scalars)
                xs[n, :, half + 2 * eb, :] = jnp.transpose(chunk)
        land_start(n, False)

    def group_sums(n, count):
        scalars = []
        sums = jnp.zeros((128, 256), F32)
        for quarter in range(4):
            turned = jnp.transpose(xr[n, :, quarter, :])
            if quarter == 0:
                scalars = take_scalars(turned, count)
            block = []
            for part in split(turned):
                row = jnp.concatenate([part[16 * e : 16 * e + 16] for e in range(8)], axis=1)
                for j in range(4):
                    block.append(row * in_owner[16 * j : 16 * j + 16, 1024 * quarter : 1024 * quarter + 1024])
            hot = hot_cam_t[1024 * quarter : 1024 * quarter + 1024, :]
            sums = sums + jnp.dot(jnp.concatenate(block, axis=0), hot, preferred_element_type=F32)
        sums = sums[0:64] + sums[64:128]
        if count:
            rows = lax.broadcasted_iota(jnp.int32, sums.shape, 0)
            sums = jnp.where(lax.bitwise_and(rows, 15) == 15, scalar_row(scalars, 256), sums)
        return sums.reshape(4, 16, 256)

    fetches[0].wait()
    fetches[1].wait()
    ag[0, cam] = padded(precondition(cam, group_rhs[cam]))
    pl.semaphore_wait(barrier, N_LAND - 1 + N_CAM - 1)
    cam_share(0)
    fetches[2].wait()
    make_hot_cam()
    for fetch in fetches[3:]:
        fetch.wait()
    make_hot_slot()
    make_jac()
    cam_wait(0, cam_recv)
    send_listed(0, 0, [])
    for n in (3, 4, 5):
        cam_share(n)
    make_land()
    make_slot_masks()
    make_cam_masks()
    land_wait(0, land_recv)
    gathered, _ = observed(0, 0)
    seen[...] = gathered
    terms, _ = eliminate(gathered)
    send_terms(1, terms, [])
    land_wait(1, land_recv)
    parts[cam] = group_sums(1, 0)
    cam_share(1)
    for n in (3, 4, 5):
        cam_wait(n, cam_recv)
    cam_wait(1, cam_recv)

    sums = [jnp.zeros((PARAMS, 256), F32)] * 4
    for j in range(N_CAM):
        start, smoothed = group_rhs[j], ag[0, j, 0:PARAMS]
        product = parts[0, j, 0:PARAMS] + parts[1, j, 0:PARAMS] + parts[2, j, 0:PARAMS] + parts[3, j, 0:PARAMS]
        product = product + group_damp[j] * smoothed
        turned = precondition(j, product)
        products[j] = product
        ag[1, j] = padded(turned)
        pairs = ((start, smoothed), (smoothed, product), (start, turned), (product, turned))
        sums = [value + left * right for value, (left, right) in zip(sums, pairs)]
    send_listed(2, 1, [total(value) for value in sums])
    land_wait(2, land_recv)
    gathered, (energy, curve, cross, square) = observed(2, 4)
    stride = energy / curve
    energy_new = energy - stride * (cross + curve) + stride * stride * square
    beta = energy_new / energy
    terms, curve = eliminate((1.0 + beta) * seen[...] - stride * gathered)
    smoothed = ag[0, cam, 0:PARAMS]
    residual = group_rhs[cam] - stride * products[cam]
    smoothed_new = smoothed - stride * ag[1, cam, 0:PARAMS]
    direction = smoothed_new + beta * smoothed
    damped = group_damp[cam] * direction
    send_terms(3, terms, [total(residual * smoothed_new), curve + total(damped * direction)])
    land_wait(3, land_recv)
    gs[...] = group_sums(3, 2)
    rr[cam] = gs[cam]
    cam_start(2, lambda peer: gs.at[peer], rr.at[cam])
    cam_wait(2, cam_recv)
    sums = rr[0] + rr[1] + rr[2] + rr[3]
    energy, curve = pick(sums[15:16], 0), pick(sums[15:16], 1)
    stride_new = energy / curve
    both_out[0] = stride * smoothed + stride_new * direction
    both_out[1] = residual - stride_new * (sums[0:PARAMS] + damped)
    for n in range(4):
        land_wait(n, land_send)
    for n in range(6):
        cam_wait(n, cam_send)


def local(jac_cam, jac_land, land_damp, obs_slot, tile_count, send_list, rhs, precond, cam_damp):
    vmem = pl.BlockSpec(memory_space=pltpu.VMEM)
    both = pl.pallas_call(
        kernel,
        out_shape=jax.ShapeDtypeStruct((2, PARAMS, 256), F32),
        in_specs=[pl.BlockSpec(memory_space=pl.ANY)] * 9,
        out_specs=vmem,
        scratch_shapes=[
            pltpu.VMEM((1, 1), jnp.int32),
            pltpu.VMEM((2, PARAMS, 4, 512), F32),
            pltpu.VMEM((2, 3, 4, 512), F32),
            pltpu.VMEM((3, 512), F32),
            pltpu.VMEM((4, 512), jnp.int32),
            pltpu.VMEM((32, 128), jnp.int32),
            pltpu.VMEM((N_CAM, PARAMS, 256), F32),
            pltpu.VMEM((N_CAM, PARAMS, PARAMS, 256), F32),
            pltpu.VMEM((N_CAM, PARAMS, 256), F32),
            pltpu.VMEM((256, 4096), BF16),
            pltpu.VMEM((256, 2048), BF16),
            pltpu.VMEM((4096, 256), BF16),
            pltpu.VMEM((2048, 256), BF16),
            pltpu.VMEM((64, 4096), BF16),
            pltpu.VMEM((256, 2048), BF16),
            pltpu.VMEM((32, 128), jnp.int32),
            pltpu.VMEM((32, 128), jnp.int32),
            pltpu.VMEM((4, 512), jnp.int32),
            pltpu.VMEM((4, 512), jnp.int32),
            pltpu.VMEM((2, 16, 2048), F32),
            pltpu.VMEM((3, 8, 512), F32),
            pltpu.VMEM((9, 512), F32),
            pltpu.VMEM((16, 2048), F32),
            pltpu.VMEM((2, 4, 16, 256), F32),
            pltpu.VMEM((N_CAM, N_CAM, 16, 256), F32),
            pltpu.VMEM((N_CAM, PARAMS, 256), F32),
            pltpu.VMEM((N_CAM, 16, 256), F32),
            pltpu.VMEM((N_CAM, 16, 256), F32),
            pltpu.VMEM((4, N_LAND, 4, 128), F32),
            pltpu.VMEM((4, N_LAND, 4, 128), F32),
            pltpu.SemaphoreType.DMA((4,)),
            pltpu.SemaphoreType.DMA((4,)),
            pltpu.SemaphoreType.DMA((6,)),
            pltpu.SemaphoreType.DMA((6,)),
            pltpu.SemaphoreType.DMA((9,)),
        ],
        compiler_params=pltpu.CompilerParams(
            collective_id=0, has_side_effects=True, vmem_limit_bytes=60 * 1024 * 1024
        ),
    )(tile_count.reshape(1, 1), jac_cam, jac_land, land_damp, obs_slot, send_list.reshape(32, 128), rhs, precond, cam_damp)
    return both[0], both[1]


def solution(mesh):
    whole = ("land", "cam")
    return jax.shard_map(
        local,
        mesh=mesh,
        in_specs=(
            P(None, None, None, whole),
            P(None, None, None, whole),
            P(None, whole),
            P(None, whole),
            P(whole),
            P(whole, None),
            P(None, whole),
            P(None, None, whole),
            P(None, whole),
        ),
        out_specs=(P(None, whole), P(None, whole)),
        check_vma=False,
    )
```
